128 devices in a mesh: row: 8 (over z_lo, x), col: 16 (over z_hi, y, core).
Axes of the slice: x: 4, y: 4, z: 4 (z_hi: 2, z_lo: 2; z = z_hi * 2 + z_lo), core: 2. Of those that a mesh axis runs over, the one named last changes fastest.
Arguments:
- single: bfloat16 [1536, 384], P('row'), may hold values from -6 to 6
- res_bin: int32 [1536, 1536], P('row', 'col'), may hold values from 0 to 65
- tok_bin: int32 [1536, 1536], P('row', 'col'), may hold values from 0 to 65
- chain_ids: int32 [1536], replicated, may hold values from 0 to 7, as said below
- w_rows: bfloat16 [384, 128], replicated, may hold values from -0.3125 to 0.3125
- w_cols: bfloat16 [384, 128], replicated, may hold values from -0.3125 to 0.3125
- rel_table: bfloat16 [138, 128], replicated, may hold values from -3 to 3
- ln_gain: float32 [128], replicated, may hold values from 0.5 to 1.5
- ln_bias: float32 [128], replicated, may hold values from -3 to 3
- w_in: bfloat16 [128, 512], replicated, may hold values from -0.5 to 0.5
- cot_ab: bfloat16 [1536, 1536, 256], P('row', 'col'), may hold values from -0.1875 to 0.1875
- cot_z: bfloat16 [1536, 1536, 128], P('row', 'col'), may hold values from -0.1875 to 0.1875
Outputs:
- grad_single: float32 [1536, 384], P('row')
- grad_w_rows: float32 [384, 128], replicated
- grad_w_cols: float32 [384, 128], replicated
- grad_table: float32 [138, 128], replicated
- grad_gain: float32 [128], replicated
- grad_bias: float32 [128], replicated
- grad_w_in: float32 [128, 512], replicated
The draws below stay inside these ranges and needn't reach their ends.
Inputs may be any that keep to these rules, and one draw needn't show every extreme that they name: `chain_ids`: token-to-chain ids of the crop: never falling along the tokens, the first token in chain 0 and the last in chain 8 - 1.
All inputs are finite; a program needn't handle non-finite values.
Results may differ from the reference program's by a relative error of at most 0.0062.
Values may be sent and summed in bfloat16 or wider, within the bound.
No kernel may reach another device: no remote copies, remote signals or barrier semaphores. Data moves between devices by JAX's collectives and lax.ppermute only.
A program may use at most 128 MiB of HBM per device.

```python
import math
import jax
import jax.numpy as jnp
from jax import lax

C_S = 384
C_Z = 128
C_H = 128
RBINS = 66
NCHAIN = 8
NBINS = 138
TOKENS = 1536


def draw_chain_ids(key, part):
    key = jax.random.fold_in(key, 7)
    breaks = jax.random.randint(key, (NCHAIN - 1,), 1, TOKENS)
    places = jnp.arange(TOKENS, dtype=jnp.int32)
    return jnp.sum((places[:, None] >= breaks[None, :]).astype(jnp.int32), axis=1)


def set_ends(entries, rng, low, top_value):
    extent = entries.shape
    spot = [jax.random.randint(jax.random.fold_in(rng, axis), (), 0, extent[axis]) for axis in range(len(extent))]
    entries = entries.at[tuple(spot)].set(low)
    longest = extent.index(max(extent))
    spot[longest] = (spot[longest] + 1) % extent[longest]
    return entries.at[tuple(spot)].set(top_value)


def level_of(stream_key, dims, shards, smallest, top_value):
    level, own = 1.0, jax.random.fold_in(stream_key, 6)
    for dim, shards_of in shards:
        steps = jnp.exp(jax.random.uniform(jax.random.fold_in(own, dim), (shards_of,), jnp.float32, smallest / len(shards), top_value / len(shards)))
        level = level * jnp.repeat(steps, dims[dim] // shards_of).reshape([-1 if axis == dim else 1 for axis in range(len(dims))])
    return level


def bell_draw(own_key, dims, scale, most, split=(), held_as=jnp.bfloat16):
    level = level_of(own_key, dims, split, -0.22, 0.18) if split else 1.0
    array = jax.random.normal(own_key, dims, jnp.float32) * scale * level
    return jnp.minimum(jnp.maximum(array, -most), most).astype(held_as)


def setup_inputs(seed: int = 0) -> dict:
    splits = jax.random.split(jax.random.key(seed), 13)
    return {
        "single": bell_draw(splits[0], (TOKENS, C_S), 1.0, 6.0, ((0, 8),)),
        "res_bin": set_ends(jax.random.randint(splits[1], (TOKENS, TOKENS), 0, RBINS), jax.random.fold_in(splits[1], 1), 0, RBINS - 1).astype(jnp.int32),
        "tok_bin": set_ends(jax.random.randint(splits[2], (TOKENS, TOKENS), 0, RBINS), jax.random.fold_in(splits[2], 1), 0, RBINS - 1).astype(jnp.int32),
        "chain_ids": draw_chain_ids(jax.random.fold_in(splits[12], 71), 0),
        "w_rows": bell_draw(splits[4], (C_S, C_Z), C_S ** -0.5, 0.3125),
        "w_cols": bell_draw(splits[5], (C_S, C_Z), C_S ** -0.5, 0.3125),
        "rel_table": bell_draw(splits[6], (NBINS, C_Z), 0.5, 3.0),
        "ln_gain": jnp.clip(1.0 + 0.1 * jax.random.normal(splits[7], (C_Z,), jnp.float32), 0.5, 1.5),
        "ln_bias": bell_draw(splits[8], (C_Z,), 0.5, 3.0, (), jnp.float32),
        "w_in": bell_draw(splits[9], (C_Z, 4 * C_H), C_Z ** -0.5, 0.5),
        "cot_ab": bell_draw(splits[10], (TOKENS, TOKENS, 2 * C_H), 0.03125, 0.1875, ((0, 8), (1, 16))),
        "cot_z": bell_draw(splits[11], (TOKENS, TOKENS, C_Z), 0.03125, 0.1875, ((0, 8), (1, 16))),
    }


def pair_features(res_rows, tok_rows, chain_left, chain_right):
    offset_bin = jnp.clip(chain_left[:, None] - chain_right[None, :] + 2, 0, 4) + 2 * RBINS
    same_bin = jnp.where(chain_left[:, None] == chain_right[None, :], 2 * RBINS + 5, -1)
    bin_ids = jnp.arange(NBINS, dtype=jnp.int32)
    multi_hot = (bin_ids == res_rows[..., None]) | (bin_ids == tok_rows[..., None] + RBINS)
    multi_hot = multi_hot | (bin_ids == offset_bin[..., None]) | (bin_ids == same_bin[..., None])
    return multi_hot.astype(jnp.float32)

def contract_rows(left, right):
    return lax.dot_general(left, right, (((0,), (0,)), ((), ())), precision=lax.Precision.HIGHEST, preferred_element_type=jnp.float32)

def block_backward(row_proj, col_proj, res_rows, tok_rows, chain_left, chain_right, cot_edges, cot_pair, rel_table, ln_gain, ln_bias, w_in):
    height = row_proj.shape[0]
    width = col_proj.shape[0]
    channels = row_proj.shape[1]
    hidden = w_in.shape[1] // 4
    flat_hot = pair_features(res_rows, tok_rows, chain_left, chain_right).reshape(height * width, -1)
    relative = jnp.dot(flat_hot.astype(jnp.bfloat16), rel_table, preferred_element_type=jnp.float32)
    relative = relative.reshape(height, width, channels)
    pair = (row_proj[:, None, :] + col_proj[None, :, :] + relative).astype(jnp.bfloat16)
    pair_wide = pair.astype(jnp.float32).reshape(height * width, channels)
    centre = lax.optimization_barrier(jnp.mean(pair_wide, axis=-1, keepdims=True))
    centred = pair_wide - centre
    variance = lax.optimization_barrier(jnp.mean(centred * centred, axis=-1, keepdims=True))
    inv_std = lax.rsqrt(variance + 1e-05)
    standard = centred * inv_std
    normed = (standard * ln_gain + ln_bias).astype(jnp.bfloat16)
    projected = jnp.dot(normed, w_in, preferred_element_type=jnp.float32)
    gate_a = projected[:, :hidden]
    value_a = projected[:, hidden:2 * hidden]
    gate_b = projected[:, 2 * hidden:3 * hidden]
    value_b = projected[:, 3 * hidden:]
    cot_wide = cot_edges.reshape(height * width, 2 * hidden).astype(jnp.float32)
    cot_a = cot_wide[:, :hidden]
    cot_b = cot_wide[:, hidden:]
    sig_a = jax.nn.sigmoid(gate_a)
    sig_b = jax.nn.sigmoid(gate_b)
    proj_grad = jnp.concatenate([cot_a * value_a * sig_a * (1.0 - sig_a), cot_a * sig_a, cot_b * value_b * sig_b * (1.0 - sig_b), cot_b * sig_b], axis=-1).astype(jnp.bfloat16)
    normed_grad = lax.dot_general(proj_grad, w_in, (((1,), (1,)), ((), ())), preferred_element_type=jnp.float32)
    grad_w_in = lax.dot_general(normed, proj_grad, (((0,), (0,)), ((), ())), preferred_element_type=jnp.float32)
    grad_gain = lax.optimization_barrier(jnp.sum(normed_grad * standard, axis=0))
    grad_bias = lax.optimization_barrier(jnp.sum(normed_grad, axis=0))
    scaled = normed_grad * ln_gain
    pair_grad = cot_pair.reshape(height * width, channels).astype(jnp.float32) + inv_std * (scaled - lax.optimization_barrier(jnp.mean(scaled, axis=-1, keepdims=True)) - standard * lax.optimization_barrier(jnp.mean(scaled * standard, axis=-1, keepdims=True)))
    grad_table = contract_rows(flat_hot, pair_grad)
    grid_grad = pair_grad.reshape(height, width, channels)
    return (grad_w_in, grad_gain, grad_bias, grad_table, lax.optimization_barrier(jnp.sum(grid_grad, axis=1)), lax.optimization_barrier(jnp.sum(grid_grad, axis=0)))

def reference(single, res_bin, tok_bin, chain_ids, w_rows, w_cols, rel_table, ln_gain, ln_bias, w_in, cot_ab, cot_z):
    proj_rows = jnp.dot(single, w_rows, preferred_element_type=jnp.float32)
    proj_cols = jnp.dot(single, w_cols, preferred_element_type=jnp.float32)
    row_step = math.gcd(TOKENS, 16)
    block_count = TOKENS // row_step

    def visit(carry, block_at):
        begin_at = (block_at * row_step).astype(jnp.int32)
        results = block_backward(lax.dynamic_slice_in_dim(proj_rows, begin_at, row_step, 0), proj_cols, lax.dynamic_slice_in_dim(res_bin, begin_at, row_step, 0), lax.dynamic_slice_in_dim(tok_bin, begin_at, row_step, 0), lax.dynamic_slice_in_dim(chain_ids, begin_at, row_step, 0), chain_ids, lax.dynamic_slice_in_dim(cot_ab, begin_at, row_step, 0), lax.dynamic_slice_in_dim(cot_z, begin_at, row_step, 0), rel_table, ln_gain, ln_bias, w_in)
        carry = (carry[0] + results[0], carry[1] + results[1], carry[2] + results[2], carry[3] + results[3], carry[4] + results[5])
        return (carry, results[4])
    zeros_init = (jnp.zeros((C_Z, 4 * C_H), jnp.float32), jnp.zeros((C_Z,), jnp.float32), jnp.zeros((C_Z,), jnp.float32), jnp.zeros((NBINS, C_Z), jnp.float32), jnp.zeros((TOKENS, C_Z), jnp.float32))
    carry, row_parts = lax.scan(visit, zeros_init, jnp.arange(block_count, dtype=jnp.int32))
    row_grad = row_parts.reshape(TOKENS, C_Z)
    col_grad = carry[4]
    singles_wide = single.astype(jnp.float32)
    grad_w_rows = contract_rows(singles_wide, row_grad)
    grad_w_cols = contract_rows(singles_wide, col_grad)
    grad_single = lax.dot_general(row_grad, w_rows.astype(jnp.float32), (((1,), (1,)), ((), ())), precision=lax.Precision.HIGHEST, preferred_element_type=jnp.float32)
    grad_single = grad_single + lax.dot_general(col_grad, w_cols.astype(jnp.float32), (((1,), (1,)), ((), ())), precision=lax.Precision.HIGHEST, preferred_element_type=jnp.float32)
    return (grad_single, grad_w_rows, grad_w_cols, carry[3], carry[1], carry[2], carry[0])
```

```python
import jax
import jax.numpy as jnp
from jax import lax
from jax.experimental import pallas as pl
from jax.experimental.pallas import tpu as pltpu
from jax.sharding import PartitionSpec as P

RBINS = 66
SLOT = 72
HOT = 2 * SLOT
NCHAIN = 8
BOTH = ("row", "col")
ROWS = 8
GROUP = 4

BF = jnp.bfloat16
F32 = jnp.float32


def dot(left, right, dims=((1,), (0,))):
    return lax.dot_general(left, right, (dims, ((), ())), preferred_element_type=F32)


def split_dot(left, right):
    high = right.astype(BF)
    low = (right - high.astype(F32)).astype(BF)
    return dot(left, high, ((0,), (0,))) + dot(left, low, ((0,), (0,)))


def pair_kernel(
    chain_left,
    bins,
    cot_ab,
    cot_z,
    single_rows,
    single_cols,
    chain_right,
    w_rows,
    w_cols,
    table,
    table_chain,
    gain_ref,
    bias_ref,
    w_in,
    sums,
    row_sums,
    col_sums,
    w_fwd,
    w_back,
    averager,
    proj_rows,
    base,
    col_acc,
    gw_acc,
    table_acc,
    gain_acc,
    bias_acc,
):
    step = pl.program_id(0)
    width = cot_z.shape[1]
    channels = cot_z.shape[2]
    hidden = channels
    gain = gain_ref[...]
    bias = bias_ref[...]

    @pl.when(step == 0)
    def _():
        wide = w_in[...].astype(F32)
        lane = lax.broadcasted_iota(jnp.int32, wide.shape, 1)
        is_gate = (lane // hidden) % 2 == 0
        w_fwd[...] = jnp.where(is_gate, wide * 0.5, wide).astype(BF)
        back = jnp.transpose(wide * jnp.where(is_gate, 0.25, 0.5))
        w_back[:, :channels] = back.astype(BF)
        mean = jnp.mean(back * gain, axis=1, keepdims=True)
        w_back[:, channels:] = jnp.broadcast_to(mean, back.shape).astype(BF)
        averager[...] = jnp.full((channels, channels), 1.0 / channels, BF)
        proj_rows[...] = dot(single_rows[...], w_rows[...])
        cols = dot(single_cols[...], w_cols[...])
        for chain in range(NCHAIN):
            offset = jnp.clip(chain - chain_right[...] + 2, 0, 4)
            value = cols
            for place in range(5):
                value = value + jnp.where(offset == place, table_chain[place : place + 1, :], 0.0)
            same = chain_right[...] == chain
            base[chain] = value + jnp.where(same, table_chain[5:6, :], 0.0)
        col_acc[...] = jnp.zeros_like(col_acc)
        gw_acc[...] = jnp.zeros_like(gw_acc)
        table_acc[...] = jnp.zeros_like(table_acc)
        gain_acc[...] = jnp.zeros_like(gain_acc)
        bias_acc[...] = jnp.zeros_like(bias_acc)

    pairs = GROUP * width
    bin_ids = lax.broadcasted_iota(jnp.int32, (SLOT, pairs), 0)
    proj_block = proj_rows[pl.ds(pl.multiple_of(step * ROWS, ROWS), ROWS), :]
    ones = averager[...]
    row_list = []
    for at in range(0, ROWS, GROUP):
        span = slice(at * width, at * width + pairs)
        res_hot = jnp.where(bin_ids == bins[0, 0:1, span], 1.0, 0.0)
        tok_hot = jnp.where(bin_ids == bins[0, 1:2, span], 1.0, 0.0)
        hot = jnp.concatenate([res_hot, tok_hot], axis=0).astype(BF)
        relative = dot(hot, table[...], ((0,), (0,))).reshape(GROUP, width, channels)
        chains = [chain_left[step * ROWS + at + k] for k in range(GROUP)]
        pair = jnp.concatenate(
            [
                relative[k] + base[chains[k]] + proj_block[at + k : at + k + 1, :]
                for k in range(GROUP)
            ],
            axis=0,
        ).astype(BF)
        centred = pair.astype(F32) - dot(pair, ones)
        variance = dot((centred * centred).astype(BF), ones)
        inv_std = lax.rsqrt(variance + 1e-05)
        standard = centred * inv_std
        normed = (standard * gain + bias).astype(BF)
        projected = dot(normed, w_fwd[...])
        parts = []
        for edge in range(2):
            begin = 2 * hidden * edge
            tanh = jnp.tanh(projected[:, begin : begin + hidden])
            value = projected[:, begin + hidden : begin + 2 * hidden]
            cot = cot_ab[at : at + GROUP, :, edge * hidden : (edge + 1) * hidden]
            cot = cot.reshape(pairs, hidden).astype(F32)
            double = cot + cot * tanh
            quad = double * value
            parts.append((quad - quad * tanh).astype(BF))
            parts.append(double.astype(BF))
        proj_grad = jnp.concatenate(parts, axis=1)
        gw_acc[...] += dot(normed, proj_grad, ((0,), (0,)))
        back = dot(proj_grad, w_back[...])
        normed_grad = back[:, :channels]
        product = normed_grad * standard
        gain_acc[...] += jnp.sum(product.reshape(pairs // 8, 8, channels), axis=0)
        bias_acc[...] += jnp.sum(normed_grad.reshape(pairs // 8, 8, channels), axis=0)
        scaled = normed_grad * gain - back[:, channels:]
        slope = dot((scaled * standard).astype(BF), ones)
        residual = cot_z[at : at + GROUP].reshape(pairs, channels).astype(F32)
        pair_grad = residual + inv_std * (scaled - standard * slope)
        table_acc[...] += dot(hot, pair_grad.astype(BF))
        grid = pair_grad.reshape(GROUP, width, channels)
        for k in range(GROUP):
            col_acc[chains[k]] += grid[k]
            row_list.append(jnp.sum(grid[k], axis=0, keepdims=True))
    row_sums[pl.ds(pl.multiple_of(step * ROWS, ROWS), ROWS), :] = jnp.concatenate(row_list, axis=0)

    @pl.when(step == pl.num_programs(0) - 1)
    def _():
        for part in range(4):
            scale = 0.25 if part % 2 == 0 else 0.5
            block = gw_acc[:, part * hidden : (part + 1) * hidden]
            sums[part * channels : (part + 1) * channels, :] = block * scale
        at = 4 * channels
        sums[at : at + HOT, :] = table_acc[...]
        total = jnp.zeros((width, channels), F32)
        places = [jnp.zeros((1, channels), F32) for _ in range(6)]
        for chain in range(NCHAIN):
            value = col_acc[chain]
            total = total + value
            offset = jnp.clip(chain - chain_right[...] + 2, 0, 4)
            for place in range(5):
                kept = jnp.where(offset == place, value, 0.0)
                places[place] = places[place] + jnp.sum(kept, axis=0, keepdims=True)
            kept = jnp.where(chain_right[...] == chain, value, 0.0)
            places[5] = places[5] + jnp.sum(kept, axis=0, keepdims=True)
        col_sums[...] = total
        for place in range(6):
            sums[at + RBINS + place : at + RBINS + place + 1, :] = places[place]
        spare = at + SLOT + RBINS
        sums[spare : spare + 1, :] = jnp.sum(gain_acc[...], axis=0, keepdims=True)
        sums[spare + 1 : spare + 2, :] = jnp.sum(bias_acc[...], axis=0, keepdims=True)
        at = at + HOT
        depth = single_rows.shape[1]
        sums[at : at + depth, :] = split_dot(single_rows[...], row_sums[...])
        at = at + depth
        sums[at : at + depth, :] = split_dot(single_cols[...], total)
        at = at + depth
        sums[at:, :] = jnp.zeros((sums.shape[0] - at, channels), F32)


def pair_work(chain_left, bins, cot_ab, cot_z, single, single_cols, chain_right, w_rows, w_cols, table, table_chain, gain, bias, w_in, padded):
    row_tok, col_tok, channels = cot_z.shape
    whole = pl.BlockSpec(memory_space=pltpu.VMEM)
    steps = row_tok // ROWS
    return pl.pallas_call(
        pair_kernel,
        grid=(steps,),
        in_specs=[
            pl.BlockSpec(memory_space=pltpu.SMEM),
            pl.BlockSpec((1, 2, ROWS * col_tok), lambda i: (i, 0, 0)),
            pl.BlockSpec((ROWS, col_tok, 2 * channels), lambda i: (i, 0, 0)),
            pl.BlockSpec((ROWS, col_tok, channels), lambda i: (i, 0, 0)),
        ]
        + [whole] * 10,
        out_specs=[whole, whole, whole],
        out_shape=[
            jax.ShapeDtypeStruct((padded, channels), F32),
            jax.ShapeDtypeStruct((row_tok, channels), F32),
            jax.ShapeDtypeStruct((col_tok, channels), F32),
        ],
        scratch_shapes=[
            pltpu.VMEM((channels, 4 * channels), BF),
            pltpu.VMEM((4 * channels, 2 * channels), BF),
            pltpu.VMEM((channels, channels), BF),
            pltpu.VMEM((row_tok, channels), F32),
            pltpu.VMEM((NCHAIN, col_tok, channels), F32),
            pltpu.VMEM((NCHAIN, col_tok, channels), F32),
            pltpu.VMEM((channels, 4 * channels), F32),
            pltpu.VMEM((HOT, channels), F32),
            pltpu.VMEM((8, channels), F32),
            pltpu.VMEM((8, channels), F32),
        ],
        compiler_params=pltpu.CompilerParams(vmem_limit_bytes=50 * 1024 * 1024),
        cost_estimate=pl.CostEstimate(
            flops=9 * 10**9, bytes_accessed=15 * 10**6, transcendentals=7 * 10**6
        ),
    )(chain_left, bins, cot_ab, cot_z, single, single_cols, chain_right, w_rows, w_cols, table, table_chain, gain, bias, w_in)


def turned(row, col):
    z_lo, x = row // 4, row % 4
    z_hi, y, core = col // 8, col // 2 % 4, col % 2
    return z_hi * 4 + y, z_lo * 8 + (x + 2) % 4 * 2 + core


def turn_pairs():
    pairs = []
    for row in range(8):
        for col in range(16):
            to_row, to_col = turned(row, col)
            pairs.append((row * 16 + col, to_row * 16 + to_col))
    return pairs


def swap(value, mask):
    return lax.ppermute(value, BOTH, [(at, at ^ mask) for at in range(128)])


def pick(value, place):
    half = value.shape[0] // 2
    return lax.dynamic_slice_in_dim(value, place * half, half, 0)


def halve(value, place, mask):
    got = swap(pick(value, 1 - place).astype(BF), mask)
    return pick(value, place) + got.astype(F32)


def both_sum(value, mask):
    return value + swap(value, mask)


def double(value, place, mask):
    got = swap(value, mask)
    first = jnp.where(place == 0, value, got)
    second = jnp.where(place == 0, got, value)
    return jnp.concatenate([first, second], axis=0)


def per_device(
    single,
    res_bin,
    tok_bin,
    chain_ids,
    w_rows,
    w_cols,
    rel_table,
    ln_gain,
    ln_bias,
    w_in,
    cot_ab,
    cot_z,
):
    row_tok, col_tok = res_bin.shape
    channels = w_rows.shape[1]
    depth = single.shape[1]
    row_at = lax.axis_index("row")
    col_at = lax.axis_index("col")
    core = col_at % 2
    y_at = col_at // 2 % 4
    y_half = (y_at % 2) ^ (y_at // 2)
    x_at = row_at % 4
    x_half = (x_at % 2) ^ (x_at // 2)
    turn = turn_pairs()

    single_cols = lax.ppermute(pick(single, core), BOTH, [(to, at) for at, to in turn])
    chain_left = lax.dynamic_slice_in_dim(chain_ids, row_at * row_tok, row_tok, 0)
    chain_right = lax.dynamic_slice_in_dim(chain_ids, col_at * col_tok, col_tok, 0)
    chain_right = jnp.broadcast_to(chain_right[:, None], (col_tok, channels))
    steps = row_tok // ROWS
    bins = jnp.stack(
        [res_bin.reshape(steps, ROWS * col_tok), tok_bin.reshape(steps, ROWS * col_tok)], axis=1
    )
    gap = jnp.zeros((SLOT - RBINS, channels), rel_table.dtype)
    table = jnp.concatenate([rel_table[:RBINS], gap, rel_table[RBINS : 2 * RBINS], gap], axis=0)
    table_chain = jnp.pad(rel_table[2 * RBINS :].astype(F32), ((0, 2), (0, 0)))
    used = 4 * channels + HOT + 2 * depth
    padded = -(-used // 128) * 128
    sums, row_sums, col_sums = pair_work(
        chain_left,
        bins,
        cot_ab,
        cot_z,
        single,
        single_cols,
        chain_right,
        w_rows,
        w_cols,
        table,
        table_chain,
        ln_gain[None, :],
        ln_bias[None, :],
        w_in,
        padded,
    )
    cols = lax.ppermute(col_sums.astype(BF), BOTH, turn).astype(F32)
    halves = jnp.concatenate([sums.reshape(2, padded // 2, channels), row_sums.reshape(2, row_tok // 2, channels)], axis=1)
    held = halve(halves.reshape(padded + row_tok, channels), core, 1)
    weights, rows = held[: padded // 2], held[padded // 2 :]
    quarter = padded // 4
    tok = row_tok // 4
    mixed = jnp.concatenate(
        [
            weights.reshape(2, quarter, channels),
            rows.reshape(2, tok, channels),
            cols.reshape(2, tok, channels),
        ],
        axis=1,
    )
    held = halve(mixed.reshape(-1, channels), y_half, 2)
    weights, tokens = halve(held[:quarter], x_half, 16), held[quarter:]
    eighth = quarter // 2
    held = jnp.concatenate([weights, tokens], axis=0)
    held = both_sum(held, 6)
    held = both_sum(held, 8)
    weights, tokens = held[:eighth], held[eighth:]
    weights = both_sum(weights, 48)
    weights = both_sum(weights, 64)
    weights = double(weights.astype(BF), x_half, 16)
    done = jnp.concatenate([weights, tokens.astype(BF)], axis=0)
    done = double(done, y_half, 2)
    done = double(done, core, 1)
    done = done.reshape(2, 2, quarter + 2 * tok, channels)
    weights = done[:, :, :quarter].reshape(padded, channels)
    rows = done[:, :, quarter : quarter + tok].reshape(row_tok, channels)
    cols = done[:, :, quarter + tok :].reshape(row_tok, channels)
    grad_single = dot(
        jnp.concatenate([rows, cols], axis=1),
        jnp.concatenate([w_rows, w_cols], axis=1),
        ((1,), (1,)),
    )
    weights = weights.astype(F32)
    at = 4 * channels
    grad_w_in = weights[:at].reshape(4, channels, channels).transpose(1, 0, 2)
    grad_w_in = grad_w_in.reshape(channels, at)
    spare = at + SLOT + RBINS
    grad_table = jnp.concatenate(
        [
            weights[at : at + RBINS],
            weights[at + SLOT : spare],
            weights[at + RBINS : at + SLOT],
        ],
        axis=0,
    )
    grad_gain = weights[spare]
    grad_bias = weights[spare + 1]
    at = at + HOT
    grad_w_rows = weights[at : at + depth]
    grad_w_cols = weights[at + depth : at + 2 * depth]
    return (grad_single, grad_w_rows, grad_w_cols, grad_table, grad_gain, grad_bias, grad_w_in)


def solution(mesh):
    in_specs = (
        P("row", None),
        P("row", "col"),
        P("row", "col"),
        P(),
        P(),
        P(),
        P(),
        P(),
        P(),
        P(),
        P("row", "col", None),
        P("row", "col", None),
    )
    out_specs = (P("row", None), P(), P(), P(), P(), P(), P())
    return jax.shard_map(
        per_device, mesh=mesh, in_specs=in_specs, out_specs=out_specs, check_vma=False
    )
```

```python
import jax
import jax.numpy as jnp
from jax import lax
from jax.experimental import pallas as pl
from jax.experimental.pallas import tpu as pltpu
from jax.sharding import PartitionSpec as P

RBINS = 66
SLOT = 72
HOT = 2 * SLOT
NCHAIN = 8
PADDED = 1536
BOTH = ("row", "col")
ROWS = 48
GROUP = 24

BF = jnp.bfloat16
F32 = jnp.float32


UNITS = "mmm"
LAG = 2


def dot(left, right, dims=((1,), (0,))):
    return lax.dot_general(left, right, (dims, ((), ())), preferred_element_type=F32)


def split_dot(left, right):
    high = right.astype(BF)
    low = (right - high.astype(F32)).astype(BF)
    return dot(left, high, ((0,), (0,))) + dot(left, low, ((0,), (0,)))


def pair_kernel(
    chain_ids,
    bins,
    cot_ab,
    cot_z,
    single_rows,
    single_cols,
    chain_right,
    w_rows,
    w_cols,
    rel_table,
    gain_ref,
    bias_ref,
    w_in,
    sums,
    row_sums,
    col_sums,
    table,
    chain_hot,
    w_fwd,
    w_back,
    averager,
    proj_rows,
    base,
    col_acc,
    gw_acc,
    table_acc,
    gain_acc,
    bias_acc,
):
    step = pl.program_id(0)
    first_row = (lax.axis_index("row") * pl.num_programs(0) + step) * ROWS
    width = cot_z.shape[1]
    channels = cot_z.shape[2]
    hidden = channels
    gain = gain_ref[...]
    bias = bias_ref[...]

    @pl.when(step == 0)
    def _():
        wide = w_in[...].astype(F32)
        lane = lax.broadcasted_iota(jnp.int32, wide.shape, 1)
        is_gate = (lane // hidden) % 2 == 0
        w_fwd[...] = jnp.where(is_gate, wide * 0.5, wide).astype(BF)
        back = jnp.transpose(wide * jnp.where(is_gate, 0.25, 0.5))
        scaled = back * gain
        w_back[:, :channels] = (scaled - jnp.mean(scaled, axis=1, keepdims=True)).astype(BF)
        w_back[:, channels:] = back.astype(BF)
        averager[...] = jnp.full((channels, channels), 1.0 / channels, BF)
        proj_rows[...] = dot(single_rows[...], w_rows[...])
        cols = dot(single_cols[...], w_cols[...])
        known = rel_table[...].astype(F32)
        gap = jnp.zeros((SLOT - RBINS, channels), F32)
        table[...] = jnp.concatenate(
            [known[:RBINS], gap, known[RBINS : 2 * RBINS], gap], axis=0
        ).astype(BF)
        lane = lax.broadcasted_iota(jnp.int32, (width, channels), 1)
        right = chain_right[...]
        is_chain = (lane == right) | (lane == right + NCHAIN)
        chain_hot[...] = jnp.where(is_chain, 1.0, 0.0).astype(BF)
        offsets = known[2 * RBINS : 2 * RBINS + 5]
        same = known[2 * RBINS + 5 :]
        nothing = jnp.zeros((1, channels), F32)
        rest = jnp.zeros((channels - 2 * NCHAIN, channels), F32)
        for chain in range(NCHAIN):
            entries = []
            for other in range(NCHAIN):
                place = min(max(chain - other + 2, 0), 4)
                entries.append(offsets[place : place + 1])
            entries += [same if other == chain else nothing for other in range(NCHAIN)]
            mixed = jnp.concatenate(entries + [rest], axis=0).astype(BF)
            base[chain] = cols + dot(chain_hot[...], mixed)
        col_acc[...] = jnp.zeros_like(col_acc)
        gw_acc[...] = jnp.zeros_like(gw_acc)
        table_acc[...] = jnp.zeros_like(table_acc)
        gain_acc[...] = jnp.zeros_like(gain_acc)
        bias_acc[...] = jnp.zeros_like(bias_acc)

    pairs = GROUP * width
    bin_ids = lax.broadcasted_iota(jnp.int32, (SLOT, pairs), 0)
    proj_block = proj_rows[pl.ds(pl.multiple_of(step * ROWS, ROWS), ROWS), :]
    ones = averager[...]
    count = ROWS // GROUP
    state = [{} for _ in range(count)]
    row_list = [None] * ROWS

    def average(value, unit):
        if unit == "x":
            return jnp.mean(value, axis=1, keepdims=True)
        return dot(value.astype(BF), ones)

    def features(now, at):
        span = slice(at * width, at * width + pairs)
        both = bins[0, 0:1, span]
        res_hot = jnp.where(bin_ids == (both & 127), 1.0, 0.0)
        tok_hot = jnp.where(bin_ids == (both >> 7), 1.0, 0.0)
        now["hot"] = jnp.concatenate([res_hot, tok_hot], axis=0).astype(BF)
        now["relative"] = dot(now["hot"], table[...], ((0,), (0,))).reshape(GROUP, width, channels)

    def initial(now, at):
        chains = [chain_ids[first_row + at + k] for k in range(GROUP)]
        now["chains"] = chains
        pair = jnp.concatenate(
            [
                now["relative"][k] + base[chains[k]] + proj_block[at + k : at + k + 1, :]
                for k in range(GROUP)
            ],
            axis=0,
        ).astype(BF)
        wide = pair.astype(F32)
        now["centred"] = wide - (average(wide, "x") if UNITS[0] == "x" else dot(pair, ones))

    def norm(now, at):
        centred = now["centred"]
        variance = average(centred * centred, UNITS[1])
        now["inv_std"] = lax.rsqrt(variance + 1e-05)
        now["standard"] = centred * now["inv_std"]
        now["normed"] = (now["standard"] * gain + bias).astype(BF)

    def gates(now, at):
        projected = dot(now["normed"], w_fwd[...])
        parts = []
        for edge in range(2):
            begin = 2 * hidden * edge
            tanh = jnp.tanh(projected[:, begin : begin + hidden])
            value = projected[:, begin + hidden : begin + 2 * hidden]
            cot = cot_ab[at : at + GROUP, :, edge * hidden : (edge + 1) * hidden]
            cot = cot.reshape(pairs, hidden).astype(F32)
            double = cot + cot * tanh
            quad = double * value
            parts.append((quad - quad * tanh).astype(BF))
            parts.append(double.astype(BF))
        now["proj_grad"] = jnp.concatenate(parts, axis=1)

    def weights(now, at):
        gw_acc[...] += dot(now["normed"], now["proj_grad"], ((0,), (0,)))
        back = dot(now["proj_grad"], w_back[...])
        standard = now["standard"]
        normed_grad = back[:, channels:]
        product = normed_grad * standard
        gain_acc[...] += jnp.sum(product.reshape(pairs // 8, 8, channels), axis=0)
        bias_acc[...] += jnp.sum(normed_grad.reshape(pairs // 8, 8, channels), axis=0)
        now["scaled"] = back[:, :channels]
        now["slope"] = average(now["scaled"] * standard, UNITS[2])

    def finish(now, at):
        residual = cot_z[at : at + GROUP].reshape(pairs, channels).astype(F32)
        pair_grad = residual + now["inv_std"] * (now["scaled"] - now["standard"] * now["slope"])
        table_acc[...] += dot(now["hot"], pair_grad.astype(BF))
        grid = pair_grad.reshape(GROUP, width, channels)
        for k in range(GROUP):
            col_acc[now["chains"][k]] += grid[k]
            row_list[at + k] = jnp.sum(grid[k], axis=0, keepdims=True)

    stages = [features, initial, norm, gates, weights, finish]
    for tick in range(count * LAG + len(stages)):
        for group in range(count):
            stage = tick - group * LAG
            if 0 <= stage < len(stages):
                stages[stage](state[group], group * GROUP)
    row_sums[pl.ds(pl.multiple_of(step * ROWS, ROWS), ROWS), :] = jnp.concatenate(row_list, axis=0)

    @pl.when(step == pl.num_programs(0) - 1)
    def _():
        for part in range(4):
            scale = 0.25 if part % 2 == 0 else 0.5
            block = gw_acc[:, part * hidden : (part + 1) * hidden]
            sums[part * channels : (part + 1) * channels, :] = block * scale
        at = 4 * channels
        sums[at : at + HOT, :] = table_acc[...]
        total = jnp.zeros((width, channels), F32)
        places = [jnp.zeros((1, channels), F32) for _ in range(6)]
        for chain in range(NCHAIN):
            value = col_acc[chain]
            total = total + value
            by_chain = split_dot(chain_hot[...], value)
            for other in range(NCHAIN):
                place = min(max(chain - other + 2, 0), 4)
                places[place] = places[place] + by_chain[other : other + 1]
            places[5] = places[5] + by_chain[chain : chain + 1]
        col_sums[...] = total
        for place in range(6):
            sums[at + RBINS + place : at + RBINS + place + 1, :] = places[place]
        spare = at + SLOT + RBINS
        sums[spare : spare + 1, :] = jnp.sum(gain_acc[...], axis=0, keepdims=True)
        sums[spare + 1 : spare + 2, :] = jnp.sum(bias_acc[...], axis=0, keepdims=True)
        at = at + HOT
        depth = single_rows.shape[1]
        sums[at : at + depth, :] = split_dot(single_rows[...], row_sums[...])
        at = at + depth
        sums[at : at + depth, :] = split_dot(single_cols[...], total)
        at = at + depth
        sums[at:, :] = jnp.zeros((sums.shape[0] - at, channels), F32)


def pair_work(chain_ids, bins, cot_ab, cot_z, *rest):
    row_tok, col_tok, channels = cot_z.shape
    steps = row_tok // ROWS

    def whole(array):
        return pl.BlockSpec(array.shape, lambda i: (0,) * array.ndim)

    results = [
        jax.ShapeDtypeStruct((PADDED, channels), F32),
        jax.ShapeDtypeStruct((row_tok, channels), F32),
        jax.ShapeDtypeStruct((col_tok, channels), F32),
    ]
    return pl.pallas_call(
        pair_kernel,
        grid=(steps,),
        in_specs=[
            pl.BlockSpec(memory_space=pltpu.SMEM),
            pl.BlockSpec((1, 1, ROWS * col_tok), lambda i: (i, 0, 0)),
            pl.BlockSpec((ROWS, col_tok, 2 * channels), lambda i: (i, 0, 0)),
            pl.BlockSpec((ROWS, col_tok, channels), lambda i: (i, 0, 0)),
        ]
        + [whole(array) for array in rest],
        out_specs=[whole(result) for result in results],
        out_shape=results,
        scratch_shapes=[
            pltpu.VMEM((HOT, channels), BF),
            pltpu.VMEM((col_tok, channels), BF),
            pltpu.VMEM((channels, 4 * channels), BF),
            pltpu.VMEM((4 * channels, 2 * channels), BF),
            pltpu.VMEM((channels, channels), BF),
            pltpu.VMEM((row_tok, channels), F32),
            pltpu.VMEM((NCHAIN, col_tok, channels), F32),
            pltpu.VMEM((NCHAIN, col_tok, channels), F32),
            pltpu.VMEM((channels, 4 * channels), F32),
            pltpu.VMEM((HOT, channels), F32),
            pltpu.VMEM((8, channels), F32),
            pltpu.VMEM((8, channels), F32),
        ],
        compiler_params=pltpu.CompilerParams(vmem_limit_bytes=50 * 1024 * 1024),
        cost_estimate=pl.CostEstimate(
            flops=9 * 10**9, bytes_accessed=15 * 10**6, transcendentals=7 * 10**6
        ),
    )(chain_ids, bins, cot_ab, cot_z, *rest)


def result_kernel(tokens, core, mine, theirs, w_rows, w_cols, *outs):
    grad_single, grad_w_rows, grad_w_cols, grad_table, grad_gain, grad_bias, grad_w_in = outs
    is_first = core[0] == 0
    channels = w_rows.shape[1]
    depth = w_rows.shape[0]
    quarter = PADDED // 4

    def fetch(low, high):
        first = jnp.where(is_first, mine[low:high], theirs[low:high])
        second = jnp.where(is_first, theirs[low:high], mine[low:high])
        return first, second

    def weights(low, high):
        pieces = []
        for part in range(4):
            begin, end = max(low - part * quarter, 0), min(high - part * quarter, quarter)
            if begin < end:
                shift = (part % 2) * (quarter + 2 * tokens)
                pieces.append(fetch(begin + shift, end + shift)[part // 2].astype(F32))
        return pieces[0] if len(pieces) == 1 else jnp.concatenate(pieces, axis=0)

    parts = []
    for kind in range(2):
        pieces = []
        for half in range(2):
            low = half * (quarter + 2 * tokens) + quarter + kind * tokens
            pieces.append(fetch(low, low + tokens))
        parts.append(jnp.concatenate([pieces[0][0], pieces[1][0], pieces[0][1], pieces[1][1]], axis=0))
    back = ((1,), (1,))
    grad_single[...] = dot(parts[0], w_rows[...], back) + dot(parts[1], w_cols[...], back)
    for part in range(4):
        at = part * channels
        grad_w_in[:, at : at + channels] = weights(at, at + channels)
    at = 4 * channels
    table = weights(at, at + HOT)
    grad_table[...] = jnp.concatenate(
        [table[:RBINS], table[SLOT : SLOT + RBINS], table[RBINS:SLOT]], axis=0
    )
    grad_gain[...] = table[SLOT + RBINS : SLOT + RBINS + 1]
    grad_bias[...] = table[SLOT + RBINS + 1 : SLOT + RBINS + 2]
    at = at + HOT
    grad_w_rows[...] = weights(at, at + depth)
    grad_w_cols[...] = weights(at + depth, at + 2 * depth)


def results(tokens, core, mine, theirs, w_rows, w_cols, row_tok):
    depth, channels = w_rows.shape
    shapes = [
        (row_tok, depth),
        (depth, channels),
        (depth, channels),
        (2 * RBINS + 6, channels),
        (1, channels),
        (1, channels),
        (channels, 4 * channels),
    ]

    def kernel(*refs):
        result_kernel(tokens, *refs)

    def whole(shape):
        return pl.BlockSpec(shape, lambda i: (0,) * len(shape))

    return pl.pallas_call(
        kernel,
        grid=(1,),
        in_specs=[pl.BlockSpec(memory_space=pltpu.SMEM)]
        + [whole(array.shape) for array in (mine, theirs, w_rows, w_cols)],
        out_specs=[whole(shape) for shape in shapes],
        out_shape=[jax.ShapeDtypeStruct(shape, F32) for shape in shapes],
        compiler_params=pltpu.CompilerParams(vmem_limit_bytes=30 * 1024 * 1024),
    )(core, mine, theirs, w_rows, w_cols)


def join_bins(res_bin, tok_bin):
    def kernel(res, tok, out):
        out[...] = res[...] + 128 * tok[...]

    return pl.pallas_call(
        kernel,
        out_shape=jax.ShapeDtypeStruct(res_bin.shape, res_bin.dtype),
        in_specs=[pl.BlockSpec(memory_space=pltpu.VMEM)] * 2,
        out_specs=pl.BlockSpec(memory_space=pltpu.VMEM),
        cost_estimate=pl.CostEstimate(flops=10**10, bytes_accessed=10**6, transcendentals=0),
    )(res_bin, tok_bin)


def turned(row, col):
    z_lo, x = row // 4, row % 4
    z_hi, y, core = col // 8, col // 2 % 4, col % 2
    return z_hi * 4 + y, z_lo * 8 + (x + 2) % 4 * 2 + core


def turn_pairs():
    pairs = []
    for row in range(8):
        for col in range(16):
            to_row, to_col = turned(row, col)
            pairs.append((row * 16 + col, to_row * 16 + to_col))
    return pairs


def swap(value, mask):
    return lax.ppermute(value, BOTH, [(at, at ^ mask) for at in range(128)])


def pick(value, place):
    half = value.shape[0] // 2
    return lax.dynamic_slice_in_dim(value, place * half, half, 0)


def halve(value, place, mask):
    got = swap(pick(value, 1 - place).astype(BF), mask)
    return pick(value, place) + got.astype(F32)


def both_sum(value, mask):
    return value + swap(value, mask)


def double(value, place, mask):
    got = swap(value, mask)
    first = jnp.where(place == 0, value, got)
    second = jnp.where(place == 0, got, value)
    return jnp.concatenate([first, second], axis=0)


def per_device(
    single,
    res_bin,
    tok_bin,
    chain_ids,
    w_rows,
    w_cols,
    rel_table,
    ln_gain,
    ln_bias,
    w_in,
    cot_ab,
    cot_z,
):
    row_tok, col_tok = res_bin.shape
    channels = w_rows.shape[1]
    row_at = lax.axis_index("row")
    col_at = lax.axis_index("col")
    core = col_at % 2
    y_at = col_at // 2 % 4
    y_half = (y_at % 2) ^ (y_at // 2)
    x_at = row_at % 4
    x_half = (x_at % 2) ^ (x_at // 2)
    turn = turn_pairs()

    single_cols = lax.ppermute(pick(single, core), BOTH, [(to, at) for at, to in turn])
    chain_right = lax.dynamic_slice_in_dim(chain_ids, col_at * col_tok, col_tok, 0)
    chain_right = jnp.broadcast_to(chain_right[:, None], (col_tok, channels))
    bins = join_bins(res_bin, tok_bin).reshape(row_tok // ROWS, 1, ROWS * col_tok)
    sums, row_sums, col_sums = pair_work(
        chain_ids,
        bins,
        cot_ab,
        cot_z,
        single,
        single_cols,
        chain_right,
        w_rows,
        w_cols,
        rel_table,
        ln_gain[None, :],
        ln_bias[None, :],
        w_in,
    )
    cols = lax.ppermute(col_sums.astype(BF), BOTH, turn).astype(F32)
    halves = jnp.concatenate(
        [
            sums.reshape(2, PADDED // 2, channels),
            row_sums.reshape(2, row_tok // 2, channels),
        ],
        axis=1,
    )
    held = halve(halves.reshape(PADDED + row_tok, channels), core, 1)
    weights, rows = held[: PADDED // 2], held[PADDED // 2 :]
    quarter = PADDED // 4
    tok = row_tok // 4
    mixed = jnp.concatenate(
        [
            weights.reshape(2, quarter, channels),
            rows.reshape(2, tok, channels),
            cols.reshape(2, tok, channels),
        ],
        axis=1,
    )
    held = halve(mixed.reshape(-1, channels), y_half, 2)
    weights, tokens = halve(held[:quarter], x_half, 16), held[quarter:]
    eighth = quarter // 2
    held = jnp.concatenate([weights, tokens], axis=0)
    held = both_sum(held, 6)
    held = both_sum(held, 8)
    weights, tokens = held[:eighth], held[eighth:]
    weights = both_sum(weights, 48)
    weights = both_sum(weights, 64)
    weights = double(weights.astype(BF), x_half, 16)
    done = jnp.concatenate([weights, tokens.astype(BF)], axis=0)
    done = double(done, y_half, 2)
    outs = results(tok, core.reshape(1), done, swap(done, 1), w_rows, w_cols, row_tok)
    grad_single, grad_w_rows, grad_w_cols, grad_table, grad_gain, grad_bias, grad_w_in = outs
    return (
        grad_single,
        grad_w_rows,
        grad_w_cols,
        grad_table,
        grad_gain.reshape(channels),
        grad_bias.reshape(channels),
        grad_w_in,
    )


def solution(mesh):
    in_specs = (
        P("row", None),
        P("row", "col"),
        P("row", "col"),
        P(),
        P(),
        P(),
        P(),
        P(),
        P(),
        P(),
        P("row", "col", None),
        P("row", "col", None),
    )
    out_specs = (P("row", None), P(), P(), P(), P(), P(), P())
    return jax.shard_map(
        per_device, mesh=mesh, in_specs=in_specs, out_specs=out_specs, check_vma=False
    )
```

```python
import jax
import jax.numpy as jnp
from jax import lax
from jax.experimental import pallas as pl
from jax.experimental.pallas import tpu as pltpu
from jax.sharding import PartitionSpec as P

RBINS = 66
SLOT = 72
HOT = 2 * SLOT
NCHAIN = 8
PADDED = 1536
BOTH = ("row", "col")
ROWS = 48
GROUP = 8

BF = jnp.bfloat16
F32 = jnp.float32


UNITS = "xmx"
LAG = 1


def dot(left, right, dims=((1,), (0,))):
    return lax.dot_general(left, right, (dims, ((), ())), preferred_element_type=F32)


def split_dot(left, right):
    high = right.astype(BF)
    low = (right - high.astype(F32)).astype(BF)
    return dot(left, high, ((0,), (0,))) + dot(left, low, ((0,), (0,)))


def pair_kernel(
    chain_ids,
    bins,
    cot_ab,
    cot_z,
    single_rows,
    single_cols,
    chain_right,
    w_rows,
    w_cols,
    rel_table,
    gain_ref,
    bias_ref,
    w_in,
    sums,
    row_sums,
    col_sums,
    table,
    chain_hot,
    w_fwd,
    w_back,
    averager,
    proj_rows,
    base,
    col_acc,
    gw_acc,
    table_acc,
    gain_acc,
    bias_acc,
):
    step = pl.program_id(0)
    first_row = (lax.axis_index("row") * pl.num_programs(0) + step) * ROWS
    width = cot_z.shape[1]
    channels = cot_z.shape[2]
    hidden = channels
    gain = gain_ref[...]
    bias = bias_ref[...]

    @pl.when(step == 0)
    def _():
        wide = w_in[...].astype(F32)
        lane = lax.broadcasted_iota(jnp.int32, wide.shape, 1)
        is_gate = (lane // hidden) % 2 == 0
        w_fwd[...] = jnp.where(is_gate, wide * 0.5, wide).astype(BF)
        back = jnp.transpose(wide * jnp.where(is_gate, 0.25, 0.5))
        scaled = back * gain
        w_back[:, :channels] = (scaled - jnp.mean(scaled, axis=1, keepdims=True)).astype(BF)
        w_back[:, channels:] = back.astype(BF)
        averager[...] = jnp.full((channels, channels), 1.0 / channels, BF)
        proj_rows[...] = dot(single_rows[...], w_rows[...])
        cols = dot(single_cols[...], w_cols[...])
        known = rel_table[...].astype(F32)
        gap = jnp.zeros((SLOT - RBINS, channels), F32)
        table[...] = jnp.concatenate(
            [known[:RBINS], gap, known[RBINS : 2 * RBINS], gap], axis=0
        ).astype(BF)
        lane = lax.broadcasted_iota(jnp.int32, (width, channels), 1)
        right = chain_right[...]
        is_chain = (lane == right) | (lane == right + NCHAIN)
        chain_hot[...] = jnp.where(is_chain, 1.0, 0.0).astype(BF)
        offsets = known[2 * RBINS : 2 * RBINS + 5]
        same = known[2 * RBINS + 5 :]
        nothing = jnp.zeros((1, channels), F32)
        rest = jnp.zeros((channels - 2 * NCHAIN, channels), F32)
        for chain in range(NCHAIN):
            entries = []
            for other in range(NCHAIN):
                place = min(max(chain - other + 2, 0), 4)
                entries.append(offsets[place : place + 1])
            entries += [same if other == chain else nothing for other in range(NCHAIN)]
            mixed = jnp.concatenate(entries + [rest], axis=0).astype(BF)
            base[chain] = cols + dot(chain_hot[...], mixed)
        col_acc[...] = jnp.zeros_like(col_acc)
        gw_acc[...] = jnp.zeros_like(gw_acc)
        table_acc[...] = jnp.zeros_like(table_acc)
        gain_acc[...] = jnp.zeros_like(gain_acc)
        bias_acc[...] = jnp.zeros_like(bias_acc)

    pairs = GROUP * width
    bin_ids = lax.broadcasted_iota(jnp.int32, (SLOT, pairs), 0)
    proj_block = proj_rows[pl.ds(pl.multiple_of(step * ROWS, ROWS), ROWS), :]
    ones = averager[...]
    count = ROWS // GROUP
    state = [{} for _ in range(count)]
    row_list = [None] * ROWS

    def average(value, unit):
        if unit == "x":
            return jnp.mean(value, axis=1, keepdims=True)
        return dot(value.astype(BF), ones)

    def features(now, at):
        span = slice(at * width, at * width + pairs)
        both = bins[0, 0:1, span]
        res_hot = jnp.where(bin_ids == (both & 127), 1.0, 0.0)
        tok_hot = jnp.where(bin_ids == (both >> 7), 1.0, 0.0)
        now["hot"] = jnp.concatenate([res_hot, tok_hot], axis=0).astype(BF)
        now["relative"] = dot(now["hot"], table[...], ((0,), (0,))).reshape(GROUP, width, channels)

    def initial(now, at):
        chains = [chain_ids[first_row + at + k] for k in range(GROUP)]
        now["chains"] = chains
        pair = jnp.concatenate(
            [
                now["relative"][k] + base[chains[k]] + proj_block[at + k : at + k + 1, :]
                for k in range(GROUP)
            ],
            axis=0,
        ).astype(BF)
        wide = pair.astype(F32)
        now["centred"] = wide - (average(wide, "x") if UNITS[0] == "x" else dot(pair, ones))

    def norm(now, at):
        centred = now["centred"]
        variance = average(centred * centred, UNITS[1])
        now["inv_std"] = lax.rsqrt(variance + 1e-05)
        now["standard"] = centred * now["inv_std"]
        now["normed"] = (now["standard"] * gain + bias).astype(BF)

    def gates(now, at):
        projected = dot(now["normed"], w_fwd[...])
        parts = []
        for edge in range(2):
            begin = 2 * hidden * edge
            tanh = jnp.tanh(projected[:, begin : begin + hidden])
            value = projected[:, begin + hidden : begin + 2 * hidden]
            cot = cot_ab[at : at + GROUP, :, edge * hidden : (edge + 1) * hidden]
            cot = cot.reshape(pairs, hidden).astype(F32)
            double = cot + cot * tanh
            quad = double * value
            parts.append((quad - quad * tanh).astype(BF))
            parts.append(double.astype(BF))
        now["proj_grad"] = jnp.concatenate(parts, axis=1)

    def weights(now, at):
        gw_acc[...] += dot(now["normed"], now["proj_grad"], ((0,), (0,)))
        back = dot(now["proj_grad"], w_back[...])
        standard = now["standard"]
        normed_grad = back[:, channels:]
        product = normed_grad * standard
        gain_acc[...] += jnp.sum(product.reshape(pairs // 8, 8, channels), axis=0)
        bias_acc[...] += jnp.sum(normed_grad.reshape(pairs // 8, 8, channels), axis=0)
        now["scaled"] = back[:, :channels]
        now["slope"] = average(now["scaled"] * standard, UNITS[2])

    def finish(now, at):
        residual = cot_z[at : at + GROUP].reshape(pairs, channels).astype(F32)
        pair_grad = residual + now["inv_std"] * (now["scaled"] - now["standard"] * now["slope"])
        table_acc[...] += dot(now["hot"], pair_grad.astype(BF))
        grid = pair_grad.reshape(GROUP, width, channels)
        for k in range(GROUP):
            col_acc[now["chains"][k]] += grid[k]
            row_list[at + k] = jnp.sum(grid[k], axis=0, keepdims=True)

    stages = [features, initial, norm, gates, weights, finish]
    for tick in range(count * LAG + len(stages)):
        for group in range(count):
            stage = tick - group * LAG
            if 0 <= stage < len(stages):
                stages[stage](state[group], group * GROUP)
    row_sums[pl.ds(pl.multiple_of(step * ROWS, ROWS), ROWS), :] = jnp.concatenate(row_list, axis=0)

    @pl.when(step == pl.num_programs(0) - 1)
    def _():
        for part in range(4):
            scale = 0.25 if part % 2 == 0 else 0.5
            block = gw_acc[:, part * hidden : (part + 1) * hidden]
            sums[part * channels : (part + 1) * channels, :] = block * scale
        at = 4 * channels
        sums[at : at + HOT, :] = table_acc[...]
        total = jnp.zeros((width, channels), F32)
        places = [jnp.zeros((1, channels), F32) for _ in range(6)]
        for chain in range(NCHAIN):
            value = col_acc[chain]
            total = total + value
            by_chain = split_dot(chain_hot[...], value)
            for other in range(NCHAIN):
                place = min(max(chain - other + 2, 0), 4)
                places[place] = places[place] + by_chain[other : other + 1]
            places[5] = places[5] + by_chain[chain : chain + 1]
        col_sums[...] = total
        for place in range(6):
            sums[at + RBINS + place : at + RBINS + place + 1, :] = places[place]
        spare = at + SLOT + RBINS
        sums[spare : spare + 1, :] = jnp.sum(gain_acc[...], axis=0, keepdims=True)
        sums[spare + 1 : spare + 2, :] = jnp.sum(bias_acc[...], axis=0, keepdims=True)
        at = at + HOT
        depth = single_rows.shape[1]
        sums[at : at + depth, :] = split_dot(single_rows[...], row_sums[...])
        at = at + depth
        sums[at : at + depth, :] = split_dot(single_cols[...], total)
        at = at + depth
        sums[at:, :] = jnp.zeros((sums.shape[0] - at, channels), F32)


def pair_work(chain_ids, bins, cot_ab, cot_z, *rest):
    row_tok, col_tok, channels = cot_z.shape
    steps = row_tok // ROWS

    def whole(array):
        return pl.BlockSpec(array.shape, lambda i: (0,) * array.ndim)

    results = [
        jax.ShapeDtypeStruct((PADDED, channels), F32),
        jax.ShapeDtypeStruct((row_tok, channels), F32),
        jax.ShapeDtypeStruct((col_tok, channels), F32),
    ]
    return pl.pallas_call(
        pair_kernel,
        grid=(steps,),
        in_specs=[
            pl.BlockSpec(memory_space=pltpu.SMEM),
            pl.BlockSpec((1, 1, ROWS * col_tok), lambda i: (i, 0, 0)),
            pl.BlockSpec((ROWS, col_tok, 2 * channels), lambda i: (i, 0, 0)),
            pl.BlockSpec((ROWS, col_tok, channels), lambda i: (i, 0, 0)),
        ]
        + [whole(array) for array in rest],
        out_specs=[whole(result) for result in results],
        out_shape=results,
        scratch_shapes=[
            pltpu.VMEM((HOT, channels), BF),
            pltpu.VMEM((col_tok, channels), BF),
            pltpu.VMEM((channels, 4 * channels), BF),
            pltpu.VMEM((4 * channels, 2 * channels), BF),
            pltpu.VMEM((channels, channels), BF),
            pltpu.VMEM((row_tok, channels), F32),
            pltpu.VMEM((NCHAIN, col_tok, channels), F32),
            pltpu.VMEM((NCHAIN, col_tok, channels), F32),
            pltpu.VMEM((channels, 4 * channels), F32),
            pltpu.VMEM((HOT, channels), F32),
            pltpu.VMEM((8, channels), F32),
            pltpu.VMEM((8, channels), F32),
        ],
        compiler_params=pltpu.CompilerParams(vmem_limit_bytes=50 * 1024 * 1024),
        cost_estimate=pl.CostEstimate(
            flops=9 * 10**9, bytes_accessed=15 * 10**6, transcendentals=7 * 10**6
        ),
    )(chain_ids, bins, cot_ab, cot_z, *rest)


def result_kernel(tokens, core, mine, theirs, w_rows, w_cols, *outs):
    grad_single, grad_w_rows, grad_w_cols, grad_table, grad_gain, grad_bias, grad_w_in = outs
    is_first = core[0] == 0
    channels = w_rows.shape[1]
    depth = w_rows.shape[0]
    half_rows = PADDED // 2

    def fetch(low, high):
        first = jnp.where(is_first, mine[low:high], theirs[low:high])
        second = jnp.where(is_first, theirs[low:high], mine[low:high])
        return first, second

    def weights(low, high):
        pieces = []
        for part in range(2):
            begin, end = max(low - part * half_rows, 0), min(high - part * half_rows, half_rows)
            if begin < end:
                pieces.append(fetch(begin, end)[part].astype(F32))
        return pieces[0] if len(pieces) == 1 else jnp.concatenate(pieces, axis=0)

    parts = []
    for kind in range(2):
        pieces = []
        for half in range(2):
            low = half_rows + half * 2 * tokens + kind * tokens
            pieces.append(fetch(low, low + tokens))
        parts.append(jnp.concatenate([pieces[0][0], pieces[1][0], pieces[0][1], pieces[1][1]], axis=0))
    back = ((1,), (1,))
    grad_single[...] = dot(parts[0], w_rows[...], back) + dot(parts[1], w_cols[...], back)
    for part in range(4):
        at = part * channels
        grad_w_in[:, at : at + channels] = weights(at, at + channels)
    at = 4 * channels
    table = weights(at, at + HOT)
    grad_table[...] = jnp.concatenate(
        [table[:RBINS], table[SLOT : SLOT + RBINS], table[RBINS:SLOT]], axis=0
    )
    grad_gain[...] = table[SLOT + RBINS : SLOT + RBINS + 1]
    grad_bias[...] = table[SLOT + RBINS + 1 : SLOT + RBINS + 2]
    at = at + HOT
    grad_w_rows[...] = weights(at, at + depth)
    grad_w_cols[...] = weights(at + depth, at + 2 * depth)


def results(tokens, core, mine, theirs, w_rows, w_cols, row_tok):
    depth, channels = w_rows.shape
    shapes = [
        (row_tok, depth),
        (depth, channels),
        (depth, channels),
        (2 * RBINS + 6, channels),
        (1, channels),
        (1, channels),
        (channels, 4 * channels),
    ]

    def kernel(*refs):
        result_kernel(tokens, *refs)

    def whole(shape):
        return pl.BlockSpec(shape, lambda i: (0,) * len(shape))

    return pl.pallas_call(
        kernel,
        grid=(1,),
        in_specs=[pl.BlockSpec(memory_space=pltpu.SMEM)]
        + [whole(array.shape) for array in (mine, theirs, w_rows, w_cols)],
        out_specs=[whole(shape) for shape in shapes],
        out_shape=[jax.ShapeDtypeStruct(shape, F32) for shape in shapes],
        compiler_params=pltpu.CompilerParams(vmem_limit_bytes=30 * 1024 * 1024),
    )(core, mine, theirs, w_rows, w_cols)


def join_bins(res_bin, tok_bin):
    def kernel(res, tok, out):
        out[...] = res[...] + 128 * tok[...]

    return pl.pallas_call(
        kernel,
        out_shape=jax.ShapeDtypeStruct(res_bin.shape, res_bin.dtype),
        in_specs=[pl.BlockSpec(memory_space=pltpu.VMEM)] * 2,
        out_specs=pl.BlockSpec(memory_space=pltpu.VMEM),
        cost_estimate=pl.CostEstimate(flops=10**10, bytes_accessed=10**6, transcendentals=0),
    )(res_bin, tok_bin)


def turned(row, col):
    z_lo, x = row // 4, row % 4
    z_hi, y, core = col // 8, col // 2 % 4, col % 2
    return z_hi * 4 + y, z_lo * 8 + (x + 2) % 4 * 2 + core


def turn_pairs():
    pairs = []
    for row in range(8):
        for col in range(16):
            to_row, to_col = turned(row, col)
            pairs.append((row * 16 + col, to_row * 16 + to_col))
    return pairs


def swap(value, mask):
    return lax.ppermute(value, BOTH, [(at, at ^ mask) for at in range(128)])


def pick(value, place):
    half = value.shape[0] // 2
    return lax.dynamic_slice_in_dim(value, place * half, half, 0)


def halve(value, place, mask):
    got = swap(pick(value, 1 - place).astype(BF), mask)
    return pick(value, place) + got.astype(F32)


def both_sum(value, mask):
    return value + swap(value, mask)


def short_sum(value, mask):
    own = lax.reduce_precision(value, 8, 7)
    return own + swap(own.astype(BF), mask).astype(F32)


def double(value, place, mask):
    got = swap(value, mask)
    first = jnp.where(place == 0, value, got)
    second = jnp.where(place == 0, got, value)
    return jnp.concatenate([first, second], axis=0)


def per_device(
    single,
    res_bin,
    tok_bin,
    chain_ids,
    w_rows,
    w_cols,
    rel_table,
    ln_gain,
    ln_bias,
    w_in,
    cot_ab,
    cot_z,
):
    row_tok, col_tok = res_bin.shape
    channels = w_rows.shape[1]
    row_at = lax.axis_index("row")
    col_at = lax.axis_index("col")
    core = col_at % 2
    y_at = col_at // 2 % 4
    y_half = (y_at % 2) ^ (y_at // 2)
    x_at = row_at % 4
    x_half = (x_at % 2) ^ (x_at // 2)
    turn = turn_pairs()

    single_cols = lax.ppermute(pick(single, core), BOTH, [(to, at) for at, to in turn])
    chain_right = lax.dynamic_slice_in_dim(chain_ids, col_at * col_tok, col_tok, 0)
    chain_right = jnp.broadcast_to(chain_right[:, None], (col_tok, channels))
    bins = join_bins(res_bin, tok_bin).reshape(row_tok // ROWS, 1, ROWS * col_tok)
    sums, row_sums, col_sums = pair_work(
        chain_ids,
        bins,
        cot_ab,
        cot_z,
        single,
        single_cols,
        chain_right,
        w_rows,
        w_cols,
        rel_table,
        ln_gain[None, :],
        ln_bias[None, :],
        w_in,
    )
    halves = jnp.concatenate(
        [
            sums.reshape(2, PADDED // 2, channels),
            row_sums.reshape(2, row_tok // 2, channels),
        ],
        axis=1,
    )
    held = halve(halves.reshape(PADDED + row_tok, channels), core, 1)
    held, col_sums = lax.optimization_barrier((held, col_sums))
    cols = lax.ppermute(col_sums.astype(BF), BOTH, turn).astype(F32)
    weights, rows = held[: PADDED // 2], held[PADDED // 2 :]
    weights = halve(weights, x_half, 16)
    eighth = PADDED // 8
    tok = row_tok // 4
    mixed = jnp.concatenate(
        [
            weights.reshape(2, eighth, channels),
            rows.reshape(2, tok, channels),
            cols.reshape(2, tok, channels),
        ],
        axis=1,
    )
    held = halve(mixed.reshape(-1, channels), y_half, 2)
    held = short_sum(held, 6)
    held = short_sum(held, 8)
    weights, tokens = held[:eighth], held[eighth:]
    weights = both_sum(weights, 48)
    weights = both_sum(weights, 64)
    done = jnp.concatenate([weights, tokens], axis=0).astype(BF)
    done = double(done, y_half, 2).reshape(2, eighth + 2 * tok, channels)
    weights = double(done[:, :eighth].reshape(2 * eighth, channels), x_half, 16)
    done = jnp.concatenate([weights, done[:, eighth:].reshape(4 * tok, channels)], axis=0)
    outs = results(tok, core.reshape(1), done, swap(done, 1), w_rows, w_cols, row_tok)
    grad_single, grad_w_rows, grad_w_cols, grad_table, grad_gain, grad_bias, grad_w_in = outs
    return (
        grad_single,
        grad_w_rows,
        grad_w_cols,
        grad_table,
        grad_gain.reshape(channels),
        grad_bias.reshape(channels),
        grad_w_in,
    )


def solution(mesh):
    in_specs = (
        P("row", None),
        P("row", "col"),
        P("row", "col"),
        P(),
        P(),
        P(),
        P(),
        P(),
        P(),
        P(),
        P("row", "col", None),
        P("row", "col", None),
    )
    out_specs = (P("row", None), P(), P(), P(), P(), P(), P())
    return jax.shard_map(
        per_device, mesh=mesh, in_specs=in_specs, out_specs=out_specs, check_vma=False
    )
```

```python
import jax
import jax.numpy as jnp
from jax import lax
from jax.experimental import pallas as pl
from jax.experimental.pallas import tpu as pltpu
from jax.sharding import PartitionSpec as P

RBINS = 66
SLOT = 72
HOT = 2 * SLOT
NCHAIN = 8
PADDED = 1536
BOTH = ("row", "col")
ROWS = 48
GROUP = 8

BF = jnp.bfloat16
F32 = jnp.float32


UNITS = "xmx"
LAG = 1


def dot(left, right, dims=((1,), (0,))):
    return lax.dot_general(left, right, (dims, ((), ())), preferred_element_type=F32)


def split_dot(left, right):
    high = right.astype(BF)
    low = (right - high.astype(F32)).astype(BF)
    return dot(left, high, ((0,), (0,))) + dot(left, low, ((0,), (0,)))


def pair_kernel(
    chain_ids,
    bins,
    cot_ab,
    cot_z,
    single_rows,
    single_cols,
    chain_right,
    w_rows,
    w_cols,
    rel_table,
    gain_ref,
    bias_ref,
    w_in,
    sums,
    row_sums,
    col_sums,
    table,
    chain_hot,
    w_fwd,
    w_back,
    averager,
    proj_rows,
    base,
    col_acc,
    gw_acc,
    table_acc,
    gain_acc,
    bias_acc,
):
    step = pl.program_id(0)
    first_row = (lax.axis_index("row") * pl.num_programs(0) + step) * ROWS
    width = cot_z.shape[1]
    channels = cot_z.shape[2]
    hidden = channels
    gain = gain_ref[...]
    bias = bias_ref[...]

    @pl.when(step == 0)
    def _():
        wide = w_in[...].astype(F32)
        lane = lax.broadcasted_iota(jnp.int32, wide.shape, 1)
        is_gate = (lane // hidden) % 2 == 0
        w_fwd[...] = jnp.where(is_gate, wide * 0.5, wide).astype(BF)
        back = jnp.transpose(wide * jnp.where(is_gate, 0.25, 0.5))
        scaled = back * gain
        w_back[:, :channels] = (scaled - jnp.mean(scaled, axis=1, keepdims=True)).astype(BF)
        w_back[:, channels:] = back.astype(BF)
        averager[...] = jnp.full((channels, channels), 1.0 / channels, BF)
        proj_rows[...] = dot(single_rows[...], w_rows[...])
        cols = dot(single_cols[...], w_cols[...])
        known = rel_table[...].astype(F32)
        gap = jnp.zeros((SLOT - RBINS, channels), F32)
        table[...] = jnp.concatenate(
            [known[:RBINS], gap, known[RBINS : 2 * RBINS], gap], axis=0
        ).astype(BF)
        lane = lax.broadcasted_iota(jnp.int32, (width, channels), 1)
        right = chain_right[...]
        is_chain = (lane == right) | (lane == right + NCHAIN)
        chain_hot[...] = jnp.where(is_chain, 1.0, 0.0).astype(BF)
        offsets = known[2 * RBINS : 2 * RBINS + 5]
        same = known[2 * RBINS + 5 :]
        nothing = jnp.zeros((1, channels), F32)
        rest = jnp.zeros((channels - 2 * NCHAIN, channels), F32)
        for chain in range(NCHAIN):
            entries = []
            for other in range(NCHAIN):
                place = min(max(chain - other + 2, 0), 4)
                entries.append(offsets[place : place + 1])
            entries += [same if other == chain else nothing for other in range(NCHAIN)]
            mixed = jnp.concatenate(entries + [rest], axis=0).astype(BF)
            base[chain] = cols + dot(chain_hot[...], mixed)
        col_acc[...] = jnp.zeros_like(col_acc)
        gw_acc[...] = jnp.zeros_like(gw_acc)
        table_acc[...] = jnp.zeros_like(table_acc)
        gain_acc[...] = jnp.zeros_like(gain_acc)
        bias_acc[...] = jnp.zeros_like(bias_acc)

    pairs = GROUP * width
    bin_ids = lax.broadcasted_iota(jnp.int32, (SLOT, pairs), 0)
    proj_block = proj_rows[pl.ds(pl.multiple_of(step * ROWS, ROWS), ROWS), :]
    ones = averager[...]
    count = ROWS // GROUP
    state = [{} for _ in range(count)]
    row_list = [None] * ROWS

    def average(value, unit):
        if unit == "x":
            return jnp.mean(value, axis=1, keepdims=True)
        return dot(value.astype(BF), ones)

    def features(now, at):
        span = slice(at * width, at * width + pairs)
        both = bins[0, 0:1, span]
        res_hot = jnp.where(bin_ids == (both & 127), 1.0, 0.0)
        tok_hot = jnp.where(bin_ids == (both >> 7), 1.0, 0.0)
        now["hot"] = jnp.concatenate([res_hot, tok_hot], axis=0).astype(BF)
        now["relative"] = dot(now["hot"], table[...], ((0,), (0,))).reshape(GROUP, width, channels)

    def initial(now, at):
        chains = [chain_ids[first_row + at + k] for k in range(GROUP)]
        now["chains"] = chains
        pair = jnp.concatenate(
            [
                now["relative"][k] + base[chains[k]] + proj_block[at + k : at + k + 1, :]
                for k in range(GROUP)
            ],
            axis=0,
        ).astype(BF)
        wide = pair.astype(F32)
        now["centred"] = wide - (average(wide, "x") if UNITS[0] == "x" else dot(pair, ones))

    def norm(now, at):
        centred = now["centred"]
        variance = average(centred * centred, UNITS[1])
        now["inv_std"] = lax.rsqrt(variance + 1e-05)
        now["standard"] = centred * now["inv_std"]
        now["normed"] = (now["standard"] * gain + bias).astype(BF)

    def gates(now, at):
        projected = dot(now["normed"], w_fwd[...])
        parts = []
        for edge in range(2):
            begin = 2 * hidden * edge
            tanh = jnp.tanh(projected[:, begin : begin + hidden])
            value = projected[:, begin + hidden : begin + 2 * hidden]
            cot = cot_ab[at : at + GROUP, :, edge * hidden : (edge + 1) * hidden]
            cot = cot.reshape(pairs, hidden).astype(F32)
            double = cot + cot * tanh
            quad = double * value
            parts.append((quad - quad * tanh).astype(BF))
            parts.append(double.astype(BF))
        now["proj_grad"] = jnp.concatenate(parts, axis=1)

    def weights(now, at):
        gw_acc[...] += dot(now["normed"], now["proj_grad"], ((0,), (0,)))
        back = dot(now["proj_grad"], w_back[...])
        standard = now["standard"]
        normed_grad = back[:, channels:]
        product = normed_grad * standard
        gain_acc[...] += jnp.sum(product.reshape(pairs // 8, 8, channels), axis=0)
        bias_acc[...] += jnp.sum(normed_grad.reshape(pairs // 8, 8, channels), axis=0)
        now["scaled"] = back[:, :channels]
        now["slope"] = average(now["scaled"] * standard, UNITS[2])

    def finish(now, at):
        residual = cot_z[at : at + GROUP].reshape(pairs, channels).astype(F32)
        pair_grad = residual + now["inv_std"] * (now["scaled"] - now["standard"] * now["slope"])
        table_acc[...] += dot(now["hot"], pair_grad.astype(BF))
        grid = pair_grad.reshape(GROUP, width, channels)
        for k in range(GROUP):
            col_acc[now["chains"][k]] += grid[k]
            row_list[at + k] = jnp.sum(grid[k], axis=0, keepdims=True)

    stages = [features, initial, norm, gates, weights, finish]
    for tick in range(count * LAG + len(stages)):
        for group in range(count):
            stage = tick - group * LAG
            if 0 <= stage < len(stages):
                stages[stage](state[group], group * GROUP)
    row_sums[pl.ds(pl.multiple_of(step * ROWS, ROWS), ROWS), :] = jnp.concatenate(row_list, axis=0)

    @pl.when(step == pl.num_programs(0) - 1)
    def _():
        for part in range(4):
            scale = 0.25 if part % 2 == 0 else 0.5
            block = gw_acc[:, part * hidden : (part + 1) * hidden]
            sums[part * channels : (part + 1) * channels, :] = block * scale
        at = 4 * channels
        sums[at : at + HOT, :] = table_acc[...]
        total = jnp.zeros((width, channels), F32)
        places = [jnp.zeros((1, channels), F32) for _ in range(6)]
        for chain in range(NCHAIN):
            value = col_acc[chain]
            total = total + value
            by_chain = split_dot(chain_hot[...], value)
            for other in range(NCHAIN):
                place = min(max(chain - other + 2, 0), 4)
                places[place] = places[place] + by_chain[other : other + 1]
            places[5] = places[5] + by_chain[chain : chain + 1]
        col_sums[...] = total
        for place in range(6):
            sums[at + RBINS + place : at + RBINS + place + 1, :] = places[place]
        spare = at + SLOT + RBINS
        sums[spare : spare + 1, :] = jnp.sum(gain_acc[...], axis=0, keepdims=True)
        sums[spare + 1 : spare + 2, :] = jnp.sum(bias_acc[...], axis=0, keepdims=True)
        at = at + HOT
        depth = single_rows.shape[1]
        sums[at : at + depth, :] = split_dot(single_rows[...], row_sums[...])
        at = at + depth
        sums[at : at + depth, :] = split_dot(single_cols[...], total)
        at = at + depth
        sums[at:, :] = jnp.zeros((sums.shape[0] - at, channels), F32)


def pair_work(chain_ids, bins, cot_ab, cot_z, *rest):
    row_tok, col_tok, channels = cot_z.shape
    steps = row_tok // ROWS

    def whole(array):
        return pl.BlockSpec(array.shape, lambda i: (0,) * array.ndim)

    results = [
        jax.ShapeDtypeStruct((PADDED, channels), F32),
        jax.ShapeDtypeStruct((row_tok, channels), F32),
        jax.ShapeDtypeStruct((col_tok, channels), F32),
    ]
    return pl.pallas_call(
        pair_kernel,
        grid=(steps,),
        in_specs=[
            pl.BlockSpec(memory_space=pltpu.SMEM),
            pl.BlockSpec((1, 1, ROWS * col_tok), lambda i: (i, 0, 0)),
            pl.BlockSpec((ROWS, col_tok, 2 * channels), lambda i: (i, 0, 0)),
            pl.BlockSpec((ROWS, col_tok, channels), lambda i: (i, 0, 0)),
        ]
        + [whole(array) for array in rest],
        out_specs=[whole(result) for result in results],
        out_shape=results,
        scratch_shapes=[
            pltpu.VMEM((HOT, channels), BF),
            pltpu.VMEM((col_tok, channels), BF),
            pltpu.VMEM((channels, 4 * channels), BF),
            pltpu.VMEM((4 * channels, 2 * channels), BF),
            pltpu.VMEM((channels, channels), BF),
            pltpu.VMEM((row_tok, channels), F32),
            pltpu.VMEM((NCHAIN, col_tok, channels), F32),
            pltpu.VMEM((NCHAIN, col_tok, channels), F32),
            pltpu.VMEM((channels, 4 * channels), F32),
            pltpu.VMEM((HOT, channels), F32),
            pltpu.VMEM((8, channels), F32),
            pltpu.VMEM((8, channels), F32),
        ],
        compiler_params=pltpu.CompilerParams(vmem_limit_bytes=50 * 1024 * 1024),
        cost_estimate=pl.CostEstimate(
            flops=9 * 10**9, bytes_accessed=15 * 10**6, transcendentals=7 * 10**6
        ),
    )(chain_ids, bins, cot_ab, cot_z, *rest)


def result_kernel(tokens, core, mine, theirs, w_rows, w_cols, *outs):
    grad_single, grad_w_rows, grad_w_cols, grad_table, grad_gain, grad_bias, grad_w_in = outs
    is_first = core[0] == 0
    channels = w_rows.shape[1]
    depth = w_rows.shape[0]
    half_rows = PADDED // 2

    def fetch(low, high):
        first = jnp.where(is_first, mine[low:high], theirs[low:high])
        second = jnp.where(is_first, theirs[low:high], mine[low:high])
        return first, second

    def weights(low, high):
        pieces = []
        for part in range(2):
            begin, end = max(low - part * half_rows, 0), min(high - part * half_rows, half_rows)
            if begin < end:
                pieces.append(fetch(begin, end)[part].astype(F32))
        return pieces[0] if len(pieces) == 1 else jnp.concatenate(pieces, axis=0)

    parts = []
    for kind in range(2):
        pieces = []
        for half in range(2):
            low = half_rows + half * 2 * tokens + kind * tokens
            pieces.append(fetch(low, low + tokens))
        parts.append(jnp.concatenate([pieces[0][0], pieces[1][0], pieces[0][1], pieces[1][1]], axis=0))
    back = ((1,), (1,))
    grad_single[...] = dot(parts[0], w_rows[...], back) + dot(parts[1], w_cols[...], back)
    for part in range(4):
        at = part * channels
        grad_w_in[:, at : at + channels] = weights(at, at + channels)
    at = 4 * channels
    table = weights(at, at + HOT)
    grad_table[...] = jnp.concatenate(
        [table[:RBINS], table[SLOT : SLOT + RBINS], table[RBINS:SLOT]], axis=0
    )
    grad_gain[...] = table[SLOT + RBINS : SLOT + RBINS + 1]
    grad_bias[...] = table[SLOT + RBINS + 1 : SLOT + RBINS + 2]
    at = at + HOT
    grad_w_rows[...] = weights(at, at + depth)
    grad_w_cols[...] = weights(at + depth, at + 2 * depth)


def results(tokens, core, mine, theirs, w_rows, w_cols, row_tok):
    depth, channels = w_rows.shape
    shapes = [
        (row_tok, depth),
        (depth, channels),
        (depth, channels),
        (2 * RBINS + 6, channels),
        (1, channels),
        (1, channels),
        (channels, 4 * channels),
    ]

    def kernel(*refs):
        result_kernel(tokens, *refs)

    def whole(shape):
        return pl.BlockSpec(shape, lambda i: (0,) * len(shape))

    return pl.pallas_call(
        kernel,
        grid=(1,),
        in_specs=[pl.BlockSpec(memory_space=pltpu.SMEM)]
        + [whole(array.shape) for array in (mine, theirs, w_rows, w_cols)],
        out_specs=[whole(shape) for shape in shapes],
        out_shape=[jax.ShapeDtypeStruct(shape, F32) for shape in shapes],
        compiler_params=pltpu.CompilerParams(vmem_limit_bytes=30 * 1024 * 1024),
    )(core, mine, theirs, w_rows, w_cols)


def join_bins(res_bin, tok_bin):
    def kernel(res, tok, out):
        out[...] = res[...] + 128 * tok[...]

    return pl.pallas_call(
        kernel,
        out_shape=jax.ShapeDtypeStruct(res_bin.shape, res_bin.dtype),
        in_specs=[pl.BlockSpec(memory_space=pltpu.VMEM)] * 2,
        out_specs=pl.BlockSpec(memory_space=pltpu.VMEM),
        cost_estimate=pl.CostEstimate(flops=10**10, bytes_accessed=10**6, transcendentals=0),
    )(res_bin, tok_bin)


def turned(row, col):
    z_lo, x = row // 4, row % 4
    z_hi, y, core = col // 8, col // 2 % 4, col % 2
    return z_hi * 4 + y, z_lo * 8 + (x + 2) % 4 * 2 + core


def turn_pairs():
    pairs = []
    for row in range(8):
        for col in range(16):
            to_row, to_col = turned(row, col)
            pairs.append((row * 16 + col, to_row * 16 + to_col))
    return pairs


def swap(value, mask):
    return lax.ppermute(value, BOTH, [(at, at ^ mask) for at in range(128)])


def pick(value, place):
    half = value.shape[0] // 2
    return lax.dynamic_slice_in_dim(value, place * half, half, 0)


def halve(value, place, mask):
    got = swap(pick(value, 1 - place).astype(BF), mask)
    return pick(value, place) + got.astype(F32)


def short_sum(value, mask):
    own = lax.reduce_precision(value, 8, 7)
    return own + swap(own.astype(BF), mask).astype(F32)


def double(value, place, mask):
    got = swap(value, mask)
    first = jnp.where(place == 0, value, got)
    second = jnp.where(place == 0, got, value)
    return jnp.concatenate([first, second], axis=0)


def per_device(
    single,
    res_bin,
    tok_bin,
    chain_ids,
    w_rows,
    w_cols,
    rel_table,
    ln_gain,
    ln_bias,
    w_in,
    cot_ab,
    cot_z,
):
    row_tok, col_tok = res_bin.shape
    channels = w_rows.shape[1]
    row_at = lax.axis_index("row")
    col_at = lax.axis_index("col")
    core = col_at % 2
    y_at = col_at // 2 % 4
    y_half = (y_at % 2) ^ (y_at // 2)
    x_at = row_at % 4
    x_half = (x_at % 2) ^ (x_at // 2)
    turn = turn_pairs()

    single_cols = lax.ppermute(pick(single, core), BOTH, [(to, at) for at, to in turn])
    chain_right = lax.dynamic_slice_in_dim(chain_ids, col_at * col_tok, col_tok, 0)
    chain_right = jnp.broadcast_to(chain_right[:, None], (col_tok, channels))
    bins = join_bins(res_bin, tok_bin).reshape(row_tok // ROWS, 1, ROWS * col_tok)
    sums, row_sums, col_sums = pair_work(
        chain_ids,
        bins,
        cot_ab,
        cot_z,
        single,
        single_cols,
        chain_right,
        w_rows,
        w_cols,
        rel_table,
        ln_gain[None, :],
        ln_bias[None, :],
        w_in,
    )
    halves = jnp.concatenate(
        [
            sums.reshape(2, PADDED // 2, channels),
            row_sums.reshape(2, row_tok // 2, channels),
        ],
        axis=1,
    )
    halves = halves.reshape(PADDED + row_tok, channels)
    held = pick(halves, core) + swap(pick(halves, 1 - core), 1)
    held, col_sums = lax.optimization_barrier((held, col_sums))
    cols = lax.ppermute(col_sums.astype(BF), BOTH, turn).astype(F32)
    weights, rows = held[: PADDED // 2], held[PADDED // 2 :]
    weights = halve(weights, x_half, 16)
    eighth = PADDED // 8
    tok = row_tok // 4
    mixed = jnp.concatenate(
        [
            weights.reshape(2, eighth, channels),
            rows.reshape(2, tok, channels),
            cols.reshape(2, tok, channels),
        ],
        axis=1,
    )
    held = halve(mixed.reshape(-1, channels), y_half, 2)
    held = short_sum(held, 6)
    held = short_sum(held, 8)
    weights, tokens = held[:eighth], held[eighth:]
    weights = short_sum(weights, 48)
    weights = short_sum(weights, 64)
    done = jnp.concatenate([weights, tokens], axis=0).astype(BF)
    done = double(done, y_half, 2).reshape(2, eighth + 2 * tok, channels)
    weights = double(done[:, :eighth].reshape(2 * eighth, channels), x_half, 16)
    done = jnp.concatenate([weights, done[:, eighth:].reshape(4 * tok, channels)], axis=0)
    outs = results(tok, core.reshape(1), done, swap(done, 1), w_rows, w_cols, row_tok)
    grad_single, grad_w_rows, grad_w_cols, grad_table, grad_gain, grad_bias, grad_w_in = outs
    return (
        grad_single,
        grad_w_rows,
        grad_w_cols,
        grad_table,
        grad_gain.reshape(channels),
        grad_bias.reshape(channels),
        grad_w_in,
    )


def solution(mesh):
    in_specs = (
        P("row", None),
        P("row", "col"),
        P("row", "col"),
        P(),
        P(),
        P(),
        P(),
        P(),
        P(),
        P(),
        P("row", "col", None),
        P("row", "col", None),
    )
    out_specs = (P("row", None), P(), P(), P(), P(), P(), P())
    return jax.shard_map(
        per_device, mesh=mesh, in_specs=in_specs, out_specs=out_specs, check_vma=False
    )
```
